32 devices in a mesh: wide: 16 (over z, y, x), narrow: 2 (over core).
Axes of the slice: x: 2, y: 2, z: 4, core: 2. Of those that a mesh axis runs over, the one named last changes fastest.
Arguments:
- patches: bfloat16 [384, 4096], P('wide', 'narrow'), may hold values from -6 to 6
- patch_index: int32 [384], P('wide'), may hold values from 0 to 255, as said below
- pos_table: bfloat16 [256, 4096], P(None, 'narrow'), may hold values from -4 to 4
- ln_gain: float32 [4096], P('narrow'), may hold values from 0.1 to 1.9
- ln_bias: float32 [4096], P('narrow'), may hold values from -0.6 to 0.6
- w_up: bfloat16 [4096, 16384], P('narrow', 'wide'), may hold values from -0.09375 to 0.09375
- up_bias: float32 [16384], P('wide'), may hold values from -3 to 3
- w_down: bfloat16 [16384, 4096], P('wide', 'narrow'), may hold values from -0.046875 to 0.046875
- d_out: bfloat16 [384, 4096], P('wide', 'narrow'), may hold values from -6 to 6
Outputs:
- d_patches: bfloat16 [384, 4096], P('wide', 'narrow')
- d_pos: float32 [256, 4096], P(None, 'narrow')
- d_gain: float32 [4096], P('narrow')
- d_lnbias: float32 [4096], P('narrow')
- d_up: bfloat16 [4096, 16384], P('narrow', 'wide')
- d_upbias: float32 [16384], P('wide')
- d_down: bfloat16 [16384, 4096], P('wide', 'narrow')
- d_downbias: float32 [4096], P('narrow')
The draws below stay inside these ranges and needn't reach their ends.
Inputs may be any that keep to these rules, and one draw needn't show every extreme that they name: `patch_index`: each aligned block of 64 tokens is one image: its patch positions are distinct, a random choice of 64 of the 256.
All inputs are finite; a program needn't handle non-finite values.
Results may differ from the reference program's by a relative error of at most 0.0062.
Values may be sent and summed in bfloat16 or wider, within the bound.
No kernel may reach another device: no remote copies, remote signals or barrier semaphores. Data moves between devices by JAX's collectives and lax.ppermute only.
A program may use at most 128 MiB of HBM per device.

```python
import jax
import jax.numpy as jnp
from jax import lax

D = 4096
FF = 16384
PATCHES = 256
VISIBLE = 64
TOKENS = 384


def draw_patch_index(key, part):
    key = jax.random.fold_in(key, 11)
    images = TOKENS // VISIBLE
    image_keys = jax.random.split(key, images)
    chosen = jax.vmap(lambda one_key: jax.random.permutation(one_key, PATCHES))(image_keys)[:, :VISIBLE]
    return chosen.reshape(-1).astype(jnp.int32)


def levels(stream_key, shape, pieces, least, high):
    gain, own = 1.0, jax.random.fold_in(stream_key, 6)
    for position, shards_of in pieces:
        draws = jnp.exp(jax.random.uniform(jax.random.fold_in(own, position), (shards_of,), jnp.float32, least / len(pieces), high / len(pieces)))
        gain = gain * jnp.repeat(draws, shape[position] // shards_of).reshape([-1 if axis == position else 1 for axis in range(len(shape))])
    return gain


def normal_values(key, shape, spread, bound, pieces=(), dtype=jnp.bfloat16):
    values = jax.random.normal(key, shape, jnp.float32) * spread
    if len(pieces) > 0:
        values = levels(key, shape, pieces, -0.22, 0.18) * values
    return jnp.clip(values, min=-bound, max=bound).astype(dtype)


def setup_inputs(seed: int = 0) -> dict:
    key_of = jax.random.split(jax.random.key(seed), 10)
    return {
        "patches": normal_values(key_of[0], (TOKENS, D), 1.0, 6.0, ((0, 16), (1, 2))),
        "patch_index": draw_patch_index(jax.random.fold_in(key_of[9], 71), 0),
        "pos_table": normal_values(key_of[2], (PATCHES, D), 0.7, 4.0, ((1, 2),)),
        "ln_gain": jnp.clip(1.0 + 0.18 * jax.random.normal(key_of[3], (D,), jnp.float32), 0.1, 1.9),
        "ln_bias": jnp.clip(jax.random.uniform(key_of[4], (D,), jnp.float32, -0.6, 0.6) * levels(key_of[4], (D,), ((0, 2),), -0.4, 0.0), -0.6, 0.6),
        "w_up": normal_values(key_of[5], (D, FF), D ** -0.5, 0.09375, ((0, 2), (1, 16))),
        "up_bias": normal_values(key_of[6], (FF,), 0.6, 3.0, ((0, 16),), jnp.float32),
        "w_down": normal_values(key_of[7], (FF, D), FF ** -0.5, 0.046875, ((0, 16), (1, 2))),
        "d_out": normal_values(key_of[8], (TOKENS, D), 1.0, 6.0, ((0, 16), (1, 2))),
    }


EPS = 1e-06
INV_ROOT_TWO = 0.7071067811865476
INV_ROOT_TWO_PI = 0.3989422804014327

def gelu_parts(values):
    normal_cdf = 0.5 * (1.0 + jax.scipy.special.erf(values * INV_ROOT_TWO))
    normal_pdf = jnp.exp(-0.5 * values * values) * INV_ROOT_TWO_PI
    return (values * normal_cdf, normal_cdf + values * normal_pdf)

def reference(patches, patch_index, pos_table, ln_gain, ln_bias, w_up, up_bias, w_down, d_out):
    layer_in = patches.astype(jnp.float32) + pos_table.astype(jnp.float32)[patch_index]
    centre_mean = lax.optimization_barrier(jnp.mean(layer_in, axis=1, keepdims=True))
    variance = lax.optimization_barrier(jnp.mean(layer_in * layer_in, axis=1, keepdims=True)) - centre_mean * centre_mean
    inverse_std = lax.rsqrt(variance + EPS)
    normed = (layer_in - centre_mean) * inverse_std
    hidden_in = (normed * ln_gain + ln_bias).astype(jnp.bfloat16)
    pre_act = jnp.dot(hidden_in, w_up, preferred_element_type=jnp.float32) + up_bias
    act_value, gelu_slope = gelu_parts(pre_act)
    activation = act_value.astype(jnp.bfloat16)
    back_grad = jnp.dot(d_out, w_down.T, preferred_element_type=jnp.float32)
    d_hidden = (back_grad * gelu_slope).astype(jnp.bfloat16)
    d_down = jnp.dot(activation.T, d_out, preferred_element_type=jnp.float32).astype(jnp.bfloat16)
    d_up = jnp.dot(hidden_in.T, d_hidden, preferred_element_type=jnp.float32).astype(jnp.bfloat16)
    d_upbias = lax.optimization_barrier(jnp.sum(d_hidden.astype(jnp.float32), axis=0))
    d_downbias = lax.optimization_barrier(jnp.sum(d_out.astype(jnp.float32), axis=0))
    d_normout = jnp.dot(d_hidden, w_up.T, preferred_element_type=jnp.float32)
    d_gain = lax.optimization_barrier(jnp.sum(d_normout * normed, axis=0))
    d_lnbias = lax.optimization_barrier(jnp.sum(d_normout, axis=0))
    scaled = d_normout * ln_gain
    d_layer = inverse_std * (scaled - lax.optimization_barrier(jnp.mean(scaled, axis=1, keepdims=True)) - normed * lax.optimization_barrier(jnp.mean(scaled * normed, axis=1, keepdims=True)))
    summed_grad = d_out.astype(jnp.float32) + d_layer
    d_patches = summed_grad.astype(jnp.bfloat16)
    d_pos = jax.ops.segment_sum(summed_grad, patch_index, num_segments=PATCHES)
    return (d_patches, d_pos, d_gain, d_lnbias, d_up, d_upbias, d_down, d_downbias)
```

```python
import jax
import jax.numpy as jnp
from jax import lax
from jax.sharding import PartitionSpec as P

D = 4096

EPS = 1e-06
INV_ROOT_TWO = 0.7071067811865476
INV_ROOT_TWO_PI = 0.3989422804014327
BF16 = jnp.bfloat16
F32 = jnp.float32


def gelu_parts(values):
    normal_cdf = 0.5 * (1.0 + jax.scipy.special.erf(values * INV_ROOT_TWO))
    normal_pdf = jnp.exp(-0.5 * values * values) * INV_ROOT_TWO_PI
    return (values * normal_cdf, normal_cdf + values * normal_pdf)


def program(wide, narrow):
    outer = wide // 4
    near = outer // 2

    def flip(x, bit):
        return lax.ppermute(x, "wide", [(i, i ^ bit) for i in range(wide)])

    def along_x(x):
        return flip(x, 1)

    def along_y(x):
        return flip(x, 2)

    def shift(x, k):
        return lax.ppermute(x, "wide", [(i, (i + 4 * k) % wide) for i in range(wide)])

    def other_core(x):
        return lax.ppermute(x, "narrow", [(0, 1), (1, 0)])

    def narrow_sum(x):
        if narrow == 2:
            return x.astype(F32) + other_core(x).astype(F32)
        return lax.psum(x.astype(F32), "narrow")

    def gather_outer(x):
        return [x] + [shift(x, k) for k in range(1, outer)]

    def gather_plane(blocks):
        low = jnp.concatenate(blocks[:near], axis=0)
        high = jnp.concatenate(blocks[near:], axis=0)
        low_x = along_x(low)
        high_y = along_y(high)
        low_y = along_y(low)
        high_x = along_x(high)
        low_xy = along_y(low_x)
        high_xy = along_x(high_y)
        return [low, high, low_x, high_x, low_y, high_y, low_xy, high_xy]

    def scatter_plane(low, high):
        low_far = along_y(low[3])
        high_far = along_x(high[3])
        low_y = along_y(low[2])
        high_x = along_x(high[1])
        low_x = along_x((low[1].astype(F32) + low_far.astype(F32)).astype(BF16))
        high_y = along_y((high[2].astype(F32) + high_far.astype(F32)).astype(BF16))
        low_sum = low[0].astype(F32) + low_y.astype(F32) + low_x.astype(F32)
        high_sum = high[0].astype(F32) + high_x.astype(F32) + high_y.astype(F32)
        return low_sum, high_sum

    def pair_sum(terms):
        while len(terms) > 1:
            half = len(terms) // 2
            terms = [terms[i] + terms[i + half] for i in range(half)]
        return terms[0]

    def on_device(patches, patch_index, pos_table, ln_gain, ln_bias, w_up, up_bias, w_down, d_out):
        rows, cols = patches.shape
        table_rows = pos_table.shape[0]
        grad_blocks = gather_outer(d_out)
        picked = lax.broadcasted_iota(jnp.int32, (rows, table_rows), 1) == patch_index[:, None]
        onehot = jnp.where(picked, 1.0, 0.0).astype(BF16)
        pos_rows = jnp.dot(onehot, pos_table, preferred_element_type=F32)
        layer_in = patches.astype(F32) + pos_rows
        sums = jnp.stack([jnp.sum(layer_in, axis=1), jnp.sum(layer_in * layer_in, axis=1)])
        first_sum, square_sum = narrow_sum(sums)
        centre_mean = (first_sum / D)[:, None]
        variance = (square_sum / D)[:, None] - centre_mean * centre_mean
        inverse_std = lax.rsqrt(variance + EPS)
        normed = (layer_in - centre_mean) * inverse_std
        hidden_in = (normed * ln_gain + ln_bias).astype(BF16)
        hidden_blocks = gather_outer(hidden_in)
        grad_panel = jnp.concatenate(gather_plane(grad_blocks), axis=0)
        hidden_panel = jnp.concatenate(gather_plane(hidden_blocks), axis=0)
        back_part = lax.dot_general(
            grad_panel, w_down, (((1,), (1,)), ((), ())), preferred_element_type=F32
        )
        pre_part = jnp.dot(hidden_panel, w_up, preferred_element_type=F32)
        back_full = narrow_sum(back_part.astype(BF16))
        pre_full = narrow_sum(pre_part.astype(BF16))
        act_value, slope = gelu_parts(pre_full + up_bias)
        activation = act_value.astype(BF16)
        d_hidden = (back_full * slope).astype(BF16)
        d_normout = lax.dot_general(
            d_hidden, w_up, (((1,), (1,)), ((), ())), preferred_element_type=F32
        ).astype(BF16)
        size = near * rows
        parts = [d_normout[i * size : (i + 1) * size] for i in range(8)]
        low_sum, high_sum = scatter_plane(parts[0::2], parts[1::2])
        plane = [low_sum[i * rows : (i + 1) * rows] for i in range(near)]
        plane += [high_sum[i * rows : (i + 1) * rows] for i in range(outer - near)]
        back_home = [shift(plane[k].astype(BF16), outer - k).astype(F32) for k in range(1, outer)]
        own_sum = pair_sum([plane[0]] + back_home)

        contract_rows = (((0,), (0,)), ((), ()))
        d_down = lax.dot_general(
            activation, grad_panel, contract_rows, preferred_element_type=F32
        ).astype(BF16)
        d_up = lax.dot_general(
            hidden_panel, d_hidden, contract_rows, preferred_element_type=F32
        ).astype(BF16)
        d_upbias = jnp.sum(d_hidden.astype(F32), axis=0)
        d_downbias = jnp.sum(grad_panel.astype(F32), axis=0)

        scaled = own_sum * ln_gain
        row_sums = narrow_sum(jnp.stack([jnp.sum(scaled, axis=1), jnp.sum(scaled * normed, axis=1)]))
        scaled_sum, cross_sum = row_sums
        d_layer = inverse_std * (
            scaled - (scaled_sum / D)[:, None] - normed * (cross_sum / D)[:, None]
        )
        summed_grad = (d_out.astype(F32) + d_layer).astype(BF16)
        gain_term = jnp.sum(own_sum * normed, axis=0)
        bias_term = jnp.sum(own_sum, axis=0)
        index_row = jnp.pad(patch_index.astype(BF16), (0, cols - rows))
        small = jnp.stack([gain_term.astype(BF16), bias_term.astype(BF16), index_row])
        payload = jnp.concatenate([summed_grad, jnp.pad(small, ((0, 5), (0, 0)))], axis=0)
        blocks = gather_outer(payload)
        pos_panel = jnp.concatenate(gather_plane([b[:rows] for b in blocks]), axis=0)
        terms = pair_sum([b[rows : rows + 2].astype(F32) for b in blocks])
        indices = jnp.concatenate([b[rows + 2, :rows] for b in blocks])

        for along in (along_x, along_y):
            tokens = indices.shape[0]
            depth = -(-tokens // cols)
            listed = jnp.pad(indices, (0, depth * cols - tokens)).reshape(depth, cols)
            packed = jnp.concatenate([terms.astype(BF16), listed], axis=0)
            other = along(packed)
            terms = packed[:2].astype(F32) + other[:2].astype(F32)
            indices = jnp.concatenate([indices, other[2:].reshape(-1)[:tokens]])
        indices = indices.astype(jnp.int32)
        d_gain, d_lnbias = terms
        owners = lax.broadcasted_iota(jnp.int32, (table_rows, indices.shape[0]), 0) == indices[None, :]
        d_pos = jnp.dot(
            jnp.where(owners, 1.0, 0.0).astype(BF16), pos_panel, preferred_element_type=F32
        )
        return (summed_grad, d_pos, d_gain, d_lnbias, d_up, d_upbias, d_down, d_downbias)

    return on_device


def solution(mesh):
    in_specs = (
        P("wide", "narrow"),
        P("wide"),
        P(None, "narrow"),
        P("narrow"),
        P("narrow"),
        P("narrow", "wide"),
        P("wide"),
        P("wide", "narrow"),
        P("wide", "narrow"),
    )
    out_specs = (
        P("wide", "narrow"),
        P(None, "narrow"),
        P("narrow"),
        P("narrow"),
        P("narrow", "wide"),
        P("wide"),
        P("wide", "narrow"),
        P("narrow"),
    )
    return jax.shard_map(
        program(mesh.shape["wide"], mesh.shape["narrow"]),
        mesh=mesh,
        in_specs=in_specs,
        out_specs=out_specs,
        check_vma=False,
    )
```

```python
import jax
import jax.numpy as jnp
from jax import lax
from jax.experimental import pallas as pl
from jax.experimental.pallas import tpu as pltpu
from jax.sharding import PartitionSpec as P

D = 4096

EPS = 1e-06
INV_ROOT_TWO = 0.7071067811865476
INV_ROOT_TWO_PI = 0.3989422804014327
BF16 = jnp.bfloat16
F32 = jnp.float32


def gelu_parts(values):
    normal_cdf = 0.5 * (1.0 + jax.scipy.special.erf(values * INV_ROOT_TWO))
    normal_pdf = jnp.exp(-0.5 * values * values) * INV_ROOT_TWO_PI
    return (values * normal_cdf, normal_cdf + values * normal_pdf)


def array(shape, dtype):
    return jax.ShapeDtypeStruct(shape, dtype)


def params():
    return pltpu.CompilerParams(vmem_limit_bytes=6 << 20)


def cost(flops, read):
    return pl.CostEstimate(flops=flops, bytes_accessed=read, transcendentals=0)


def once(shape):
    return pl.BlockSpec(shape, lambda i: (0, 0), pipeline_mode=pl.Buffered(1))


def place_kernel(*refs):
    pieces, indices, d_pos = refs[:4], *refs[4:]
    shape = (d_pos.shape[0], indices.shape[1])
    owners = lax.broadcasted_iota(jnp.int32, shape, 0) == indices[...]
    rows = jnp.concatenate([piece[...] for piece in pieces])
    d_pos[...] = jnp.dot(
        jnp.where(owners, 1.0, 0.0).astype(BF16), rows, preferred_element_type=F32
    )


def place(pieces, indices, places):
    size, cols = pieces[0].shape
    tile = min(cols, 512)
    return pl.pallas_call(
        place_kernel,
        grid=(cols // tile,),
        out_shape=array((places, cols), F32),
        in_specs=[pl.BlockSpec((size, tile), lambda i: (0, i))] * 4 + [once((1, 4 * size))],
        out_specs=pl.BlockSpec((places, tile), lambda i: (0, i)),
        compiler_params=params(),
        cost_estimate=cost(8 * size * places * cols, 8 * size * cols),
        name="place",
    )(*pieces, indices)


def program(wide, narrow):
    outer = wide // 4

    def flip(x, bits):
        return lax.ppermute(x, "wide", [(i, i ^ bits) for i in range(wide)])

    def turn(x, step):
        bits = [((1, 2), (2, 1))[c if narrow == 2 else 0][step] for c in range(narrow)]
        pairs = [
            (i * narrow + c, (i ^ bits[c]) * narrow + c) for i in range(wide) for c in range(narrow)
        ]
        return lax.ppermute(x, ("wide", "narrow"), pairs)

    def other_core(x):
        return lax.ppermute(x, "narrow", [(0, 1), (1, 0)])

    def narrow_sum(x):
        if narrow == 2:
            return x.astype(F32) + other_core(x).astype(F32)
        return lax.psum(x.astype(F32), "narrow")

    def narrow_sum_tokens(x):
        if narrow != 2:
            return narrow_sum(x)
        got, size = other_core(x), x.shape[0] // 4
        quarters = [got[i * size : (i + 1) * size] for i in (0, 2, 1, 3)]
        return x.astype(F32) + jnp.concatenate(quarters).astype(F32)

    def gather(own, rider=None):
        column = jnp.concatenate([own] + [flip(own, 4 * k) for k in range(1, outer)])
        first, second = lax.optimization_barrier((turn(column, 0), turn(column, 1)))
        both = turn(first, 1)
        if rider is not None:
            for step in range(outer.bit_length() - 1):
                rider += flip(rider, 4 << step)
            rider, _ = lax.optimization_barrier((rider, column))
            rider += turn(rider, 0)
            rider, _ = lax.optimization_barrier((rider, first))
            rider += turn(rider, 1)
        return (column, first, second, both), rider

    def order():
        core = lax.axis_index("narrow") if narrow == 2 else 0
        quarters = jnp.where(core == 0, jnp.array([0, 1, 2, 3]), jnp.array([0, 2, 1, 3]))
        patterns = quarters[:, None] + 4 * jnp.arange(outer)[None]
        return jnp.bitwise_xor(lax.axis_index("wide"), patterns.reshape(-1))

    def on_device(patches, patch_index, pos_table, ln_gain, ln_bias, w_up, up_bias, w_down, d_out):
        rows, cols = patches.shape
        table_rows = pos_table.shape[0]
        picked = lax.broadcasted_iota(jnp.int32, (rows, table_rows), 1) == patch_index[:, None]
        onehot = jnp.where(picked, 1.0, 0.0).astype(BF16)
        pos_rows = jnp.dot(onehot, pos_table, preferred_element_type=F32)
        layer_in = patches.astype(F32) + pos_rows
        sums = jnp.stack([jnp.sum(layer_in, axis=1), jnp.sum(layer_in * layer_in, axis=1)])
        first_sum, square_sum = narrow_sum(sums)
        centre_mean = (first_sum / D)[:, None]
        variance = (square_sum / D)[:, None] - centre_mean * centre_mean
        inverse_std = lax.rsqrt(variance + EPS)
        normed = (layer_in - centre_mean) * inverse_std
        hidden_in = (normed * ln_gain + ln_bias).astype(BF16)
        grad_panel = jnp.concatenate(gather(d_out)[0])
        hidden_panel = jnp.concatenate(gather(hidden_in)[0])
        back_part = lax.dot_general(
            grad_panel, w_down, (((1,), (1,)), ((), ())), preferred_element_type=F32
        )
        pre_part = jnp.dot(hidden_panel, w_up, preferred_element_type=F32)
        back_full = narrow_sum_tokens(back_part.astype(BF16))
        pre_full = narrow_sum_tokens(pre_part.astype(BF16))
        act_value, slope = gelu_parts(pre_full + up_bias)
        activation = act_value.astype(BF16)
        d_hidden = (back_full * slope).astype(BF16)
        d_normout = lax.dot_general(
            d_hidden, w_up, (((1,), (1,)), ((), ())), preferred_element_type=F32
        ).astype(BF16)
        size = outer * rows
        parts = [d_normout[i * size : (i + 1) * size] for i in range(4)]
        own, first, second, both = parts
        far, near = turn(both, 1), turn(second, 1)
        back = turn((first.astype(F32) + far.astype(F32)).astype(BF16), 0)
        activation, grad_panel, _ = lax.optimization_barrier((activation, grad_panel, far))
        contract_rows = (((0,), (0,)), ((), ()))
        d_down = lax.dot_general(
            activation, grad_panel, contract_rows, preferred_element_type=F32
        ).astype(BF16)
        d_downbias = jnp.sum(grad_panel.astype(F32), axis=0)
        back, d_down, d_downbias = lax.optimization_barrier((back, d_down, d_downbias))
        column = own.astype(F32) + near.astype(F32) + back.astype(F32)
        blocks = [column[i * rows : (i + 1) * rows] for i in range(outer)]
        home = [flip(blocks[k].astype(BF16), 4 * k) for k in range(1, outer)]
        d_hidden, hidden_panel, _ = lax.optimization_barrier((d_hidden, hidden_panel, back))
        d_up = lax.dot_general(
            hidden_panel, d_hidden, contract_rows, preferred_element_type=F32
        ).astype(BF16)
        d_upbias = jnp.sum(d_hidden.astype(F32), axis=0)
        d_up, d_upbias, home = lax.optimization_barrier((d_up, d_upbias, home))
        own_sum = sum([block.astype(F32) for block in home], blocks[0])

        scaled = own_sum * ln_gain
        row_sums = narrow_sum(jnp.stack([jnp.sum(scaled, axis=1), jnp.sum(scaled * normed, axis=1)]))
        scaled_sum, cross_sum = row_sums
        d_layer = inverse_std * (
            scaled - (scaled_sum / D)[:, None] - normed * (cross_sum / D)[:, None]
        )
        summed_grad = (d_out.astype(F32) + d_layer).astype(BF16)
        gain_term = jnp.sum(own_sum * normed, axis=0)
        bias_term = jnp.sum(own_sum, axis=0)
        tokens = wide * rows
        depth = -(-tokens // cols)
        lane = lax.broadcasted_iota(jnp.int32, (wide, rows), 0)
        mine = jnp.where(lane == lax.axis_index("wide"), patch_index.astype(F32)[None], 0.0)
        mine = jnp.pad(mine.reshape(-1), (0, depth * cols - tokens)).reshape(depth, cols)
        rider = jnp.concatenate([jnp.stack([gain_term, bias_term]), mine])
        pos_pieces, rider = gather(summed_grad, rider)
        d_gain, d_lnbias = rider[0], rider[1]
        indices = rider[2:].reshape(-1)[:tokens].astype(jnp.int32).reshape(wide, rows)
        indices = jnp.take(indices, order(), axis=0, mode="clip").reshape(-1)
        d_pos = place(pos_pieces, indices[None], table_rows)
        return (summed_grad, d_pos, d_gain, d_lnbias, d_up, d_upbias, d_down, d_downbias)

    return on_device


def solution(mesh):
    in_specs = (
        P("wide", "narrow"),
        P("wide"),
        P(None, "narrow"),
        P("narrow"),
        P("narrow"),
        P("narrow", "wide"),
        P("wide"),
        P("wide", "narrow"),
        P("wide", "narrow"),
    )
    out_specs = (
        P("wide", "narrow"),
        P(None, "narrow"),
        P("narrow"),
        P("narrow"),
        P("narrow", "wide"),
        P("wide"),
        P("wide", "narrow"),
        P("narrow"),
    )
    return jax.shard_map(
        program(mesh.shape["wide"], mesh.shape["narrow"]),
        mesh=mesh,
        in_specs=in_specs,
        out_specs=out_specs,
        check_vma=False,
    )
```

```python
import jax
import jax.numpy as jnp
from jax import lax
from jax.experimental import pallas as pl
from jax.experimental.pallas import tpu as pltpu
from jax.sharding import PartitionSpec as P

D = 4096

EPS = 1e-06
INV_ROOT_TWO = 0.7071067811865476
INV_ROOT_TWO_PI = 0.3989422804014327
BF16 = jnp.bfloat16
F32 = jnp.float32


def gelu_parts(values):
    normal_cdf = 0.5 * (1.0 + jax.scipy.special.erf(values * INV_ROOT_TWO))
    normal_pdf = jnp.exp(-0.5 * values * values) * INV_ROOT_TWO_PI
    return (values * normal_cdf, normal_cdf + values * normal_pdf)


def array(shape, dtype):
    return jax.ShapeDtypeStruct(shape, dtype)


def params():
    return pltpu.CompilerParams(vmem_limit_bytes=6 << 20)


def cost(flops, read):
    return pl.CostEstimate(flops=flops, bytes_accessed=read, transcendentals=0)


def once(shape):
    return pl.BlockSpec(shape, lambda i: (0, 0), pipeline_mode=pl.Buffered(1))


def place_kernel(*refs):
    pieces, indices, d_pos = refs[:4], *refs[4:]
    shape = (d_pos.shape[0], indices.shape[1])
    owners = lax.broadcasted_iota(jnp.int32, shape, 0) == indices[...]
    rows = jnp.concatenate([piece[...] for piece in pieces])
    d_pos[...] = jnp.dot(
        jnp.where(owners, 1.0, 0.0).astype(BF16), rows, preferred_element_type=F32
    )


def place(pieces, indices, places):
    size, cols = pieces[0].shape
    tile = min(cols, 512)
    return pl.pallas_call(
        place_kernel,
        grid=(cols // tile,),
        out_shape=array((places, cols), F32),
        in_specs=[pl.BlockSpec((size, tile), lambda i: (0, i))] * 4 + [once((1, 4 * size))],
        out_specs=pl.BlockSpec((places, tile), lambda i: (0, i)),
        compiler_params=params(),
        cost_estimate=cost(8 * size * places * cols, 8 * size * cols),
        name="place",
    )(*pieces, indices)


def program(wide, narrow):
    outer = wide // 4

    def flip(x, bits):
        return lax.ppermute(x, "wide", [(i, i ^ bits) for i in range(wide)])

    def turn(x, step):
        bits = [((1, 2), (2, 1))[c if narrow == 2 else 0][step] for c in range(narrow)]
        pairs = [
            (i * narrow + c, (i ^ bits[c]) * narrow + c) for i in range(wide) for c in range(narrow)
        ]
        return lax.ppermute(x, ("wide", "narrow"), pairs)

    def other_core(x):
        return lax.ppermute(x, "narrow", [(0, 1), (1, 0)])

    def narrow_sum(x):
        if narrow == 2:
            return x.astype(F32) + other_core(x).astype(F32)
        return lax.psum(x.astype(F32), "narrow")

    def narrow_sum_tokens(x):
        if narrow != 2:
            return narrow_sum(x)
        got, size = other_core(x), x.shape[0] // 4
        quarters = [got[i * size : (i + 1) * size] for i in (0, 2, 1, 3)]
        return x.astype(F32) + jnp.concatenate(quarters).astype(F32)

    def gather(own, rider=None, beside=None, ahead=None):
        later, _ = lax.optimization_barrier((own, ahead))
        along = [flip(own if k < 3 else later, 4 * k) for k in range(1, outer)]
        if beside is not None:
            along, beside = lax.optimization_barrier((along, beside))
        column = jnp.concatenate([own] + along)
        first, second = lax.optimization_barrier((turn(column, 0), turn(column, 1)))
        both = turn(first, 1)
        if rider is not None:
            for step in range(outer.bit_length() - 1):
                rider += flip(rider, 4 << step)
            rider, _ = lax.optimization_barrier((rider, column))
            rider += turn(rider, 0)
            rider, _ = lax.optimization_barrier((rider, first))
            rider += turn(rider, 1)
        return (column, first, second, both), rider, beside

    def order():
        core = lax.axis_index("narrow") if narrow == 2 else 0
        quarters = jnp.where(core == 0, jnp.array([0, 1, 2, 3]), jnp.array([0, 2, 1, 3]))
        patterns = quarters[:, None] + 4 * jnp.arange(outer)[None]
        return jnp.bitwise_xor(lax.axis_index("wide"), patterns.reshape(-1))

    def on_device(patches, patch_index, pos_table, ln_gain, ln_bias, w_up, up_bias, w_down, d_out):
        rows, cols = patches.shape
        table_rows = pos_table.shape[0]
        picked = lax.broadcasted_iota(jnp.int32, (rows, table_rows), 1) == patch_index[:, None]
        onehot = jnp.where(picked, 1.0, 0.0).astype(BF16)
        pos_rows = jnp.dot(onehot, pos_table, preferred_element_type=F32)
        layer_in = patches.astype(F32) + pos_rows
        sums = jnp.stack([jnp.sum(layer_in, axis=1), jnp.sum(layer_in * layer_in, axis=1)])
        first_sum, square_sum = narrow_sum(sums)
        centre_mean = (first_sum / D)[:, None]
        variance = (square_sum / D)[:, None] - centre_mean * centre_mean
        inverse_std = lax.rsqrt(variance + EPS)
        normed = (layer_in - centre_mean) * inverse_std
        hidden_in = (normed * ln_gain + ln_bias).astype(BF16)
        grad_panel = jnp.concatenate(gather(d_out, ahead=sums)[0])
        hidden_panel = jnp.concatenate(gather(hidden_in)[0])
        back_part = lax.dot_general(
            grad_panel, w_down, (((1,), (1,)), ((), ())), preferred_element_type=F32
        )
        pre_part = jnp.dot(hidden_panel, w_up, preferred_element_type=F32)
        back_full = narrow_sum_tokens(back_part.astype(BF16))
        pre_full = narrow_sum_tokens(pre_part.astype(BF16))
        act_value, slope = gelu_parts(pre_full + up_bias)
        activation = act_value.astype(BF16)
        d_hidden = (back_full * slope).astype(BF16)

        def norm_grads(d_hidden):
            return lax.dot_general(
                d_hidden, w_up, (((1,), (1,)), ((), ())), preferred_element_type=F32
            ).astype(BF16)

        size = outer * rows
        both = norm_grads(d_hidden[3 * size :])
        others = norm_grads(d_hidden[: 3 * size])
        own, first, second = [others[i * size : (i + 1) * size] for i in range(3)]
        far, near = turn(both, 1), turn(second, 1)
        back = turn((first.astype(F32) + far.astype(F32)).astype(BF16), 0)
        activation, grad_panel, _ = lax.optimization_barrier((activation, grad_panel, far))
        contract_rows = (((0,), (0,)), ((), ()))
        d_down = lax.dot_general(
            activation, grad_panel, contract_rows, preferred_element_type=F32
        ).astype(BF16)
        back, d_down = lax.optimization_barrier((back, d_down))
        grad_panel, _ = lax.optimization_barrier((grad_panel, back))
        d_downbias = jnp.sum(grad_panel.astype(F32), axis=0)
        column = own.astype(F32) + near.astype(F32) + back.astype(F32)
        blocks = [column[i * rows : (i + 1) * rows] for i in range(outer)]
        blocks[1:] = [block.astype(BF16) for block in blocks[1:]]
        later, _ = lax.optimization_barrier((blocks, d_downbias))
        home = [flip((blocks if k < 3 else later)[k], 4 * k) for k in range(1, outer)]
        own_sum = sum([block.astype(F32) for block in home], blocks[0])

        scaled = own_sum * ln_gain
        row_sums = narrow_sum(jnp.stack([jnp.sum(scaled, axis=1), jnp.sum(scaled * normed, axis=1)]))
        scaled_sum, cross_sum = row_sums
        d_layer = inverse_std * (
            scaled - (scaled_sum / D)[:, None] - normed * (cross_sum / D)[:, None]
        )
        summed_grad = (d_out.astype(F32) + d_layer).astype(BF16)
        gain_term = jnp.sum(own_sum * normed, axis=0)
        bias_term = jnp.sum(own_sum, axis=0)
        tokens = wide * rows
        depth = -(-tokens // cols)
        lane = lax.broadcasted_iota(jnp.int32, (wide, rows), 0)
        mine = jnp.where(lane == lax.axis_index("wide"), patch_index.astype(F32)[None], 0.0)
        mine = jnp.pad(mine.reshape(-1), (0, depth * cols - tokens)).reshape(depth, cols)
        rider = jnp.concatenate([jnp.stack([gain_term, bias_term]), mine])
        d_hidden, hidden_panel, summed_grad = lax.optimization_barrier((d_hidden, hidden_panel, summed_grad))
        d_up = lax.dot_general(
            hidden_panel, d_hidden, contract_rows, preferred_element_type=F32
        ).astype(BF16)
        d_upbias = jnp.sum(d_hidden.astype(F32), axis=0)
        rider, _ = lax.optimization_barrier((rider, summed_grad))
        pos_pieces, rider, (d_up, d_upbias) = gather(summed_grad, rider, (d_up, d_upbias))
        d_gain, d_lnbias = rider[0], rider[1]
        indices = rider[2:].reshape(-1)[:tokens].astype(jnp.int32).reshape(wide, rows)
        indices = jnp.take(indices, order(), axis=0, mode="clip").reshape(-1)
        d_pos = place(pos_pieces, indices[None], table_rows)
        return (summed_grad, d_pos, d_gain, d_lnbias, d_up, d_upbias, d_down, d_downbias)

    return on_device


def solution(mesh):
    in_specs = (
        P("wide", "narrow"),
        P("wide"),
        P(None, "narrow"),
        P("narrow"),
        P("narrow"),
        P("narrow", "wide"),
        P("wide"),
        P("wide", "narrow"),
        P("wide", "narrow"),
    )
    out_specs = (
        P("wide", "narrow"),
        P(None, "narrow"),
        P("narrow"),
        P("narrow"),
        P("narrow", "wide"),
        P("wide"),
        P("wide", "narrow"),
        P("narrow"),
    )
    return jax.shard_map(
        program(mesh.shape["wide"], mesh.shape["narrow"]),
        mesh=mesh,
        in_specs=in_specs,
        out_specs=out_specs,
        check_vma=False,
    )
```

```python
import jax
import jax.numpy as jnp
from jax import lax
from jax.experimental import pallas as pl
from jax.experimental.pallas import tpu as pltpu
from jax.sharding import PartitionSpec as P

D = 4096

EPS = 1e-06
INV_ROOT_TWO = 0.7071067811865476
INV_ROOT_TWO_PI = 0.3989422804014327
BF16 = jnp.bfloat16
F32 = jnp.float32


def gelu_parts(values):
    normal_cdf = 0.5 * (1.0 + jax.scipy.special.erf(values * INV_ROOT_TWO))
    normal_pdf = jnp.exp(-0.5 * values * values) * INV_ROOT_TWO_PI
    return (values * normal_cdf, normal_cdf + values * normal_pdf)


def array(shape, dtype):
    return jax.ShapeDtypeStruct(shape, dtype)


def params():
    return pltpu.CompilerParams(vmem_limit_bytes=6 << 20)


def cost(flops, read):
    return pl.CostEstimate(flops=flops, bytes_accessed=read, transcendentals=0)


def once(shape):
    return pl.BlockSpec(shape, lambda i: (0, 0), pipeline_mode=pl.Buffered(1))


def place_kernel(*refs):
    pieces, indices, d_pos = refs[:4], *refs[4:]
    shape = (d_pos.shape[0], indices.shape[1])
    owners = lax.broadcasted_iota(jnp.int32, shape, 0) == indices[...]
    rows = jnp.concatenate([piece[...] for piece in pieces])
    d_pos[...] = jnp.dot(
        jnp.where(owners, 1.0, 0.0).astype(BF16), rows, preferred_element_type=F32
    )


def place(pieces, indices, places):
    size, cols = pieces[0].shape
    tile = min(cols, 512)
    return pl.pallas_call(
        place_kernel,
        grid=(cols // tile,),
        out_shape=array((places, cols), F32),
        in_specs=[pl.BlockSpec((size, tile), lambda i: (0, i))] * 4 + [once((1, 4 * size))],
        out_specs=pl.BlockSpec((places, tile), lambda i: (0, i)),
        compiler_params=params(),
        cost_estimate=cost(8 * size * places * cols, 8 * size * cols),
        name="place",
    )(*pieces, indices)


def program(wide, narrow):
    outer = wide // 4

    def flip(x, bits):
        return lax.ppermute(x, "wide", [(i, i ^ bits) for i in range(wide)])

    def turn(x, step):
        bits = [((1, 2), (2, 1))[c if narrow == 2 else 0][step] for c in range(narrow)]
        pairs = [
            (i * narrow + c, (i ^ bits[c]) * narrow + c) for i in range(wide) for c in range(narrow)
        ]
        return lax.ppermute(x, ("wide", "narrow"), pairs)

    def other_core(x):
        return lax.ppermute(x, "narrow", [(0, 1), (1, 0)])

    def narrow_sum(x):
        if narrow == 2:
            return x.astype(F32) + other_core(x).astype(F32)
        return lax.psum(x.astype(F32), "narrow")

    def narrow_sum_tokens(x):
        if narrow != 2:
            return narrow_sum(x)
        got, size = other_core(x), x.shape[0] // 4
        quarters = [got[i * size : (i + 1) * size] for i in (0, 2, 1, 3)]
        return x.astype(F32) + jnp.concatenate(quarters).astype(F32)

    def gather(own, rider=None, beside=None, ahead=None):
        later, _ = lax.optimization_barrier((own, ahead))
        along = [flip(own if k < 3 else later, 4 * k) for k in range(1, outer)]
        if beside is not None:
            along, beside = lax.optimization_barrier((along, beside))
        column = jnp.concatenate([own] + along)
        first, second = lax.optimization_barrier((turn(column, 0), turn(column, 1)))
        both = turn(first, 1)
        if rider is not None:
            for step in range(outer.bit_length() - 1):
                rider += flip(rider, 4 << step)
            rider, _ = lax.optimization_barrier((rider, column))
            rider += turn(rider, 0)
            rider, _ = lax.optimization_barrier((rider, first))
            rider += turn(rider, 1)
        return (column, first, second, both), rider, beside

    def order():
        core = lax.axis_index("narrow") if narrow == 2 else 0
        quarters = jnp.where(core == 0, jnp.array([0, 1, 2, 3]), jnp.array([0, 2, 1, 3]))
        patterns = quarters[:, None] + 4 * jnp.arange(outer)[None]
        return jnp.bitwise_xor(lax.axis_index("wide"), patterns.reshape(-1))

    def on_device(patches, patch_index, pos_table, ln_gain, ln_bias, w_up, up_bias, w_down, d_out):
        rows, cols = patches.shape
        table_rows = pos_table.shape[0]
        picked = lax.broadcasted_iota(jnp.int32, (rows, table_rows), 1) == patch_index[:, None]
        onehot = jnp.where(picked, 1.0, 0.0).astype(BF16)
        pos_rows = jnp.dot(onehot, pos_table, preferred_element_type=F32)
        layer_in = patches.astype(F32) + pos_rows
        sums = jnp.stack([jnp.sum(layer_in, axis=1), jnp.sum(layer_in * layer_in, axis=1)])
        first_sum, square_sum = narrow_sum(sums)
        centre_mean = (first_sum / D)[:, None]
        variance = (square_sum / D)[:, None] - centre_mean * centre_mean
        inverse_std = lax.rsqrt(variance + EPS)
        normed = (layer_in - centre_mean) * inverse_std
        hidden_in = (normed * ln_gain + ln_bias).astype(BF16)
        grad_panel = jnp.concatenate(gather(d_out, ahead=sums)[0])
        hidden_panel = jnp.concatenate(gather(hidden_in)[0])
        back_part = lax.dot_general(
            grad_panel, w_down, (((1,), (1,)), ((), ())), preferred_element_type=F32
        )
        pre_part = jnp.dot(hidden_panel, w_up, preferred_element_type=F32)
        back_full = narrow_sum_tokens(back_part.astype(BF16))
        pre_full = narrow_sum_tokens(pre_part.astype(BF16))
        act_value, slope = gelu_parts(pre_full + up_bias)
        activation = act_value.astype(BF16)
        d_hidden = (back_full * slope).astype(BF16)

        def norm_grads(d_hidden):
            return lax.dot_general(
                d_hidden, w_up, (((1,), (1,)), ((), ())), preferred_element_type=F32
            ).astype(BF16)

        size = outer * rows
        both = norm_grads(d_hidden[3 * size :])
        others = norm_grads(d_hidden[: 3 * size])
        own, first, second = [others[i * size : (i + 1) * size] for i in range(3)]
        far, near = turn(both, 1), turn(second, 1)
        back = turn((first.astype(F32) + far.astype(F32)).astype(BF16), 0)
        activation, grad_panel, _ = lax.optimization_barrier((activation, grad_panel, far))
        contract_rows = (((0,), (0,)), ((), ()))
        d_down = lax.dot_general(
            activation, grad_panel, contract_rows, preferred_element_type=F32
        ).astype(BF16)
        d_downbias = jnp.sum(grad_panel.astype(F32), axis=0)
        back, d_down, d_downbias = lax.optimization_barrier((back, d_down, d_downbias))
        column = own.astype(F32) + near.astype(F32) + back.astype(F32)
        blocks = [column[i * rows : (i + 1) * rows] for i in range(outer)]
        blocks[1:] = [block.astype(BF16) for block in blocks[1:]]
        later, _ = lax.optimization_barrier((blocks, d_downbias))
        home = [flip((blocks if k < 3 else later)[k], 4 * k) for k in range(1, outer)]
        own_sum = sum([block.astype(F32) for block in home], blocks[0])

        scaled = own_sum * ln_gain
        row_sums = narrow_sum(jnp.stack([jnp.sum(scaled, axis=1), jnp.sum(scaled * normed, axis=1)]))
        scaled_sum, cross_sum = row_sums
        d_layer = inverse_std * (
            scaled - (scaled_sum / D)[:, None] - normed * (cross_sum / D)[:, None]
        )
        summed_grad = (d_out.astype(F32) + d_layer).astype(BF16)
        gain_term = jnp.sum(own_sum * normed, axis=0)
        bias_term = jnp.sum(own_sum, axis=0)
        tokens = wide * rows
        depth = -(-tokens // cols)
        lane = lax.broadcasted_iota(jnp.int32, (wide, rows), 0)
        mine = jnp.where(lane == lax.axis_index("wide"), patch_index.astype(F32)[None], 0.0)
        mine = jnp.pad(mine.reshape(-1), (0, depth * cols - tokens)).reshape(depth, cols)
        rider = jnp.concatenate([jnp.stack([gain_term, bias_term]), mine])
        d_hidden, hidden_panel, summed_grad = lax.optimization_barrier((d_hidden, hidden_panel, summed_grad))
        d_up = lax.dot_general(
            hidden_panel, d_hidden, contract_rows, preferred_element_type=F32
        ).astype(BF16)
        d_upbias = jnp.sum(d_hidden.astype(F32), axis=0)
        rider, _ = lax.optimization_barrier((rider, summed_grad))
        pos_pieces, rider, (d_up, d_upbias) = gather(summed_grad, rider, (d_up, d_upbias))
        d_gain, d_lnbias = rider[0], rider[1]
        indices = rider[2:].reshape(-1)[:tokens].astype(jnp.int32).reshape(wide, rows)
        indices = jnp.take(indices, order(), axis=0, mode="clip").reshape(-1)
        d_pos = place(pos_pieces, indices[None], table_rows)
        return (summed_grad, d_pos, d_gain, d_lnbias, d_up, d_upbias, d_down, d_downbias)

    return on_device


def solution(mesh):
    in_specs = (
        P("wide", "narrow"),
        P("wide"),
        P(None, "narrow"),
        P("narrow"),
        P("narrow"),
        P("narrow", "wide"),
        P("wide"),
        P("wide", "narrow"),
        P("wide", "narrow"),
    )
    out_specs = (
        P("wide", "narrow"),
        P(None, "narrow"),
        P("narrow"),
        P("narrow"),
        P("narrow", "wide"),
        P("wide"),
        P("wide", "narrow"),
        P("narrow"),
    )
    return jax.shard_map(
        program(mesh.shape["wide"], mesh.shape["narrow"]),
        mesh=mesh,
        in_specs=in_specs,
        out_specs=out_specs,
        check_vma=False,
    )
```

```python
import jax
import jax.numpy as jnp
from jax import lax
from jax.experimental import pallas as pl
from jax.experimental.pallas import tpu as pltpu
from jax.sharding import PartitionSpec as P

D = 4096

EPS = 1e-06
INV_ROOT_TWO = 0.7071067811865476
INV_ROOT_TWO_PI = 0.3989422804014327
BF16 = jnp.bfloat16
F32 = jnp.float32


def gelu_parts(values):
    normal_cdf = 0.5 * (1.0 + jax.scipy.special.erf(values * INV_ROOT_TWO))
    normal_pdf = jnp.exp(-0.5 * values * values) * INV_ROOT_TWO_PI
    return (values * normal_cdf, normal_cdf + values * normal_pdf)


def array(shape, dtype):
    return jax.ShapeDtypeStruct(shape, dtype)


def params():
    return pltpu.CompilerParams(vmem_limit_bytes=10 << 20)


def cost(flops, read):
    return pl.CostEstimate(flops=flops, bytes_accessed=read, transcendentals=0)


def once(shape):
    return pl.BlockSpec(shape, lambda i: (0, 0), pipeline_mode=pl.Buffered(1))


def place_kernel(*refs):
    pieces, indices, d_pos = refs[:4], *refs[4:]
    shape = (d_pos.shape[0], indices.shape[1])
    owners = lax.broadcasted_iota(jnp.int32, shape, 0) == indices[...]
    rows = jnp.concatenate([piece[...] for piece in pieces])
    d_pos[...] = jnp.dot(
        jnp.where(owners, 1.0, 0.0).astype(BF16), rows, preferred_element_type=F32
    )


def place(pieces, indices, places):
    size, cols = pieces[0].shape
    tile = min(cols, 1024)
    return pl.pallas_call(
        place_kernel,
        grid=(cols // tile,),
        out_shape=array((places, cols), F32),
        in_specs=[pl.BlockSpec((size, tile), lambda i: (0, i))] * 4 + [once((1, 4 * size))],
        out_specs=pl.BlockSpec((places, tile), lambda i: (0, i)),
        compiler_params=params(),
        cost_estimate=cost(8 * size * places * cols, 8 * size * cols),
        name="place",
    )(*pieces, indices)


def program(wide, narrow):
    outer = wide // 4

    def flip(x, bits):
        return lax.ppermute(x, "wide", [(i, i ^ bits) for i in range(wide)])

    def turn(x, step):
        bits = [((1, 2), (2, 1))[c if narrow == 2 else 0][step] for c in range(narrow)]
        pairs = [
            (i * narrow + c, (i ^ bits[c]) * narrow + c) for i in range(wide) for c in range(narrow)
        ]
        return lax.ppermute(x, ("wide", "narrow"), pairs)

    def other_core(x):
        return lax.ppermute(x, "narrow", [(0, 1), (1, 0)])

    def narrow_sum(x):
        if narrow == 2:
            return x.astype(F32) + other_core(x).astype(F32)
        return lax.psum(x.astype(F32), "narrow")

    def narrow_sum_tokens(x):
        if narrow != 2:
            return narrow_sum(x)
        got, size = other_core(x), x.shape[0] // 4
        quarters = [got[i * size : (i + 1) * size] for i in (0, 2, 1, 3)]
        return x.astype(F32) + jnp.concatenate(quarters).astype(F32)

    def gather(own, rider=None, beside=None, ahead=None):
        later, _ = lax.optimization_barrier((own, ahead))
        along = [flip(own if k < 3 else later, 4 * k) for k in range(1, outer)]
        if beside is not None:
            along, beside = lax.optimization_barrier((along, beside))
        column = jnp.concatenate([own] + along)
        first, second = lax.optimization_barrier((turn(column, 0), turn(column, 1)))
        both = turn(first, 1)
        if rider is not None:
            for step in range(outer.bit_length() - 1):
                rider += flip(rider, 4 << step)
            rider, _ = lax.optimization_barrier((rider, column))
            rider += turn(rider, 0)
            rider, _ = lax.optimization_barrier((rider, first))
            rider += turn(rider, 1)
        return (column, first, second, both), rider, beside

    def order():
        core = lax.axis_index("narrow") if narrow == 2 else 0
        quarters = jnp.where(core == 0, jnp.array([0, 1, 2, 3]), jnp.array([0, 2, 1, 3]))
        patterns = quarters[:, None] + 4 * jnp.arange(outer)[None]
        return jnp.bitwise_xor(lax.axis_index("wide"), patterns.reshape(-1))

    def on_device(patches, patch_index, pos_table, ln_gain, ln_bias, w_up, up_bias, w_down, d_out):
        rows, cols = patches.shape
        table_rows = pos_table.shape[0]
        picked = lax.broadcasted_iota(jnp.int32, (rows, table_rows), 1) == patch_index[:, None]
        onehot = jnp.where(picked, 1.0, 0.0).astype(BF16)
        pos_rows = jnp.dot(onehot, pos_table, preferred_element_type=F32)
        layer_in = patches.astype(F32) + pos_rows
        sums = jnp.stack([jnp.sum(layer_in, axis=1), jnp.sum(layer_in * layer_in, axis=1)])
        first_sum, square_sum = narrow_sum(sums)
        centre_mean = (first_sum / D)[:, None]
        variance = (square_sum / D)[:, None] - centre_mean * centre_mean
        inverse_std = lax.rsqrt(variance + EPS)
        normed = (layer_in - centre_mean) * inverse_std
        hidden_in = (normed * ln_gain + ln_bias).astype(BF16)
        grad_panel = jnp.concatenate(gather(d_out, ahead=sums)[0])
        hidden_panel = jnp.concatenate(gather(hidden_in)[0])
        back_part = lax.dot_general(
            grad_panel, w_down, (((1,), (1,)), ((), ())), preferred_element_type=F32
        )
        pre_part = jnp.dot(hidden_panel, w_up, preferred_element_type=F32)
        back_full = narrow_sum_tokens(back_part.astype(BF16))
        pre_full = narrow_sum_tokens(pre_part.astype(BF16))
        act_value, slope = gelu_parts(pre_full + up_bias)
        activation = act_value.astype(BF16)
        d_hidden = (back_full * slope).astype(BF16)

        def norm_grads(d_hidden):
            return lax.dot_general(
                d_hidden, w_up, (((1,), (1,)), ((), ())), preferred_element_type=F32
            ).astype(BF16)

        size = outer * rows
        both = norm_grads(d_hidden[3 * size :])
        others = norm_grads(d_hidden[: 3 * size])
        own, first, second = [others[i * size : (i + 1) * size] for i in range(3)]
        far, near = turn(both, 1), turn(second, 1)
        back = turn((first.astype(F32) + far.astype(F32)).astype(BF16), 0)
        activation, grad_panel, _ = lax.optimization_barrier((activation, grad_panel, far))
        contract_rows = (((0,), (0,)), ((), ()))
        d_down = lax.dot_general(
            activation, grad_panel, contract_rows, preferred_element_type=F32
        ).astype(BF16)
        d_downbias = jnp.sum(grad_panel.astype(F32), axis=0)
        back, d_down, d_downbias = lax.optimization_barrier((back, d_down, d_downbias))
        column = own.astype(F32) + near.astype(F32) + back.astype(F32)
        blocks = [column[i * rows : (i + 1) * rows] for i in range(outer)]
        blocks[1:] = [block.astype(BF16) for block in blocks[1:]]
        later, _ = lax.optimization_barrier((blocks, d_downbias))
        home = [flip((blocks if k < 3 else later)[k], 4 * k) for k in range(1, outer)]
        own_sum = sum([block.astype(F32) for block in home], blocks[0])

        scaled = own_sum * ln_gain
        row_sums = narrow_sum(jnp.stack([jnp.sum(scaled, axis=1), jnp.sum(scaled * normed, axis=1)]))
        scaled_sum, cross_sum = row_sums
        d_layer = inverse_std * (
            scaled - (scaled_sum / D)[:, None] - normed * (cross_sum / D)[:, None]
        )
        summed_grad = (d_out.astype(F32) + d_layer).astype(BF16)
        gain_term = jnp.sum(own_sum * normed, axis=0)
        bias_term = jnp.sum(own_sum, axis=0)
        tokens = wide * rows
        depth = -(-tokens // cols)
        lane = lax.broadcasted_iota(jnp.int32, (wide, rows), 0)
        mine = jnp.where(lane == lax.axis_index("wide"), patch_index.astype(F32)[None], 0.0)
        mine = jnp.pad(mine.reshape(-1), (0, depth * cols - tokens)).reshape(depth, cols)
        rider = jnp.concatenate([jnp.stack([gain_term, bias_term]), mine])
        d_hidden, hidden_panel, summed_grad = lax.optimization_barrier((d_hidden, hidden_panel, summed_grad))
        d_up = lax.dot_general(
            hidden_panel, d_hidden, contract_rows, preferred_element_type=F32
        ).astype(BF16)
        d_upbias = jnp.sum(d_hidden.astype(F32), axis=0)
        rider, _ = lax.optimization_barrier((rider, summed_grad))
        pos_pieces, rider, (d_up, d_upbias) = gather(summed_grad, rider, (d_up, d_upbias))
        d_gain, d_lnbias = rider[0], rider[1]
        indices = rider[2:].reshape(-1)[:tokens].astype(jnp.int32).reshape(wide, rows)
        indices = jnp.take(indices, order(), axis=0, mode="clip").reshape(-1)
        d_pos = place(pos_pieces, indices[None], table_rows)
        return (summed_grad, d_pos, d_gain, d_lnbias, d_up, d_upbias, d_down, d_downbias)

    return on_device


def solution(mesh):
    in_specs = (
        P("wide", "narrow"),
        P("wide"),
        P(None, "narrow"),
        P("narrow"),
        P("narrow"),
        P("narrow", "wide"),
        P("wide"),
        P("wide", "narrow"),
        P("wide", "narrow"),
    )
    out_specs = (
        P("wide", "narrow"),
        P(None, "narrow"),
        P("narrow"),
        P("narrow"),
        P("narrow", "wide"),
        P("wide"),
        P("wide", "narrow"),
        P("narrow"),
    )
    return jax.shard_map(
        program(mesh.shape["wide"], mesh.shape["narrow"]),
        mesh=mesh,
        in_specs=in_specs,
        out_specs=out_specs,
        check_vma=False,
    )
```
